32 devices in a mesh: groups: 2 (over y), dp: 4 (over z), mp: 4 (over x, core).
Axes of the slice: x: 2, y: 2, z: 4, core: 2. Of those that a mesh axis runs over, the one named last changes fastest.
Arguments:
- layer_input: bfloat16 [8192, 4096], P(('groups', 'dp'), 'mp'), parts along dimension 0, may hold values from -6 to 6
- output_grad: bfloat16 [8192, 4096], P(('groups', 'dp'), 'mp'), parts along dimension 0, may hold values from -6 to 6
- gate_preact: bfloat16 [8192, 11008], P(('groups', 'dp'), 'mp'), parts along dimension 0, may hold values from -6 to 6
- up_values: bfloat16 [8192, 11008], P(('groups', 'dp'), 'mp'), parts along dimension 0, may hold values from -6 to 6
- down_weight: bfloat16 [11008, 4096], P('mp', 'dp'), may hold values from -0.09375 to 0.09375
- up_in_factor: bfloat16 [4096, 64], P('mp'), may hold values from -0.09375 to 0.09375
- up_out_factor: bfloat16 [11008, 64], P('mp'), may hold values from -0.0546875 to 0.0546875
- down_in_factor: bfloat16 [11008, 64], P('mp'), may hold values from -0.0546875 to 0.0546875
- down_out_factor: bfloat16 [4096, 64], P('mp'), may hold values from -0.09375 to 0.09375
- queries: bfloat16 [64, 8192], P(('groups', 'dp')), parts along dimension 0, may hold values from -0.005859375 to 0.005859375
Outputs:
- scores: float32 [32, 32], P(('groups', 'dp')), parts along dimension 0
The draws below stay inside these ranges and needn't reach their ends.
There are 2 independent parts, one for each index of `groups`. The reference program is written for one: setup_inputs(seed, part) draws one part's arguments, and reference() takes and returns one part's arrays. A program takes and returns all parts, laid end to end along the dimension named above; an argument that names none is the same for every part. Nothing has to cross between parts.
All inputs are finite; a program needn't handle non-finite values.
Results may differ from the reference program's by a relative error of at most 0.0042.
Values may be sent and summed in bfloat16 or wider, within the bound.
A program may use at most 128 MiB of HBM per device.

```python
import jax
import jax.numpy as jnp
from jax import lax

D = 4096
FF = 11008
R = 64
SEQ = 256
TOKENS = 4096
QUERIES = 32


def block_levels(own_key, dims, pieces, least, largest):
    gain, own = 1.0, jax.random.fold_in(own_key, 6)
    for position, parts in pieces:
        heights = jnp.exp(jax.random.uniform(jax.random.fold_in(own, position), (parts,), jnp.float32, least / len(pieces), largest / len(pieces)))
        gain = gain * jnp.repeat(heights, dims[position] // parts).reshape([-1 if axis == position else 1 for axis in range(len(dims))])
    return gain


def gaussian(key, extent, scale, bound, shards=(), dtype=jnp.bfloat16):
    level = block_levels(key, extent, shards, -0.22, 0.18) if shards else 1.0
    values = jax.random.normal(key, extent, jnp.float32) * scale * level
    return jnp.minimum(jnp.maximum(values, -bound), bound).astype(dtype)


def setup_inputs(seed: int = 0, part: int = 0) -> dict:
    keys = jax.random.split(jax.random.key(seed), 11)
    part_keys = jax.random.split(jax.random.fold_in(keys[10], part), 11)
    layer_input = gaussian(part_keys[0], (TOKENS, D), 1.0, 6.0, ((0, 4), (1, 4)))
    output_grad = gaussian(part_keys[1], (TOKENS, D), 1.0, 6.0, ((0, 4), (1, 4)))
    gate_preact = gaussian(part_keys[2], (TOKENS, FF), 1.0, 6.0, ((0, 4), (1, 4)))
    up_values = gaussian(part_keys[3], (TOKENS, FF), 1.0, 6.0, ((0, 4), (1, 4)))
    down_weight = gaussian(keys[4], (FF, D), D ** -0.5, 0.09375, ((0, 4), (1, 4)))
    up_in_factor = gaussian(keys[5], (D, R), D ** -0.5, 0.09375, ((0, 4),))
    up_out_factor = gaussian(keys[6], (FF, R), FF ** -0.5, 0.0546875, ((0, 4),))
    down_in_factor = gaussian(keys[7], (FF, R), FF ** -0.5, 0.0546875, ((0, 4),))
    down_out_factor = gaussian(keys[8], (D, R), D ** -0.5, 0.09375, ((0, 4),))
    queries = gaussian(part_keys[9], (QUERIES, 2 * R * R), (R * R * SEQ) ** -0.5, 0.005859375, ((0, 4),))
    return dict(layer_input=layer_input, output_grad=output_grad, gate_preact=gate_preact, up_values=up_values, down_weight=down_weight, up_in_factor=up_in_factor, up_out_factor=up_out_factor, down_in_factor=down_in_factor, down_out_factor=down_out_factor, queries=queries)


def reference(layer_input, output_grad, gate_preact, up_values, down_weight, up_in_factor, up_out_factor, down_in_factor, down_out_factor, queries):
    silu_gate = jax.nn.silu(gate_preact.astype(jnp.float32))
    hidden = (silu_gate * up_values.astype(jnp.float32)).astype(jnp.bfloat16)
    back = jnp.dot(output_grad, down_weight.T, preferred_element_type=jnp.float32)
    up_grad = (back * silu_gate).astype(jnp.bfloat16)
    in_up = jnp.dot(layer_input, up_in_factor, preferred_element_type=jnp.float32)
    out_up = jnp.dot(up_grad, up_out_factor, preferred_element_type=jnp.float32)
    in_down = jnp.dot(hidden, down_in_factor, preferred_element_type=jnp.float32)
    out_down = jnp.dot(output_grad, down_out_factor, preferred_element_type=jnp.float32)
    count = TOKENS // SEQ
    sketch_up = jnp.einsum("nti,ntj->nij", in_up.reshape(count, SEQ, R), out_up.reshape(count, SEQ, R), precision=lax.Precision.HIGHEST)
    sketch_down = jnp.einsum("nti,ntj->nij", in_down.reshape(count, SEQ, R), out_down.reshape(count, SEQ, R), precision=lax.Precision.HIGHEST)
    sketch = jnp.concatenate([sketch_up.reshape(count, R * R), sketch_down.reshape(count, R * R)], 1).astype(jnp.bfloat16)
    return jnp.dot(sketch, queries.T, preferred_element_type=jnp.float32)
```

```python
import functools

import jax
import jax.numpy as jnp
from jax import lax
from jax.experimental import pallas as pl
from jax.experimental.pallas import tpu as pltpu
from jax.sharding import PartitionSpec as P

SEQ = 256
PIECES = 4
MESH = pl.DeviceIdType.MESH
NT = (((1,), (1,)), ((), ()))


def cuts(total, parts):
    units = -(-total // 128)
    parts = min(parts, units)
    edges = [min(total, 128 * ((units * i + parts - 1) // parts)) for i in range(parts + 1)]
    return [(a, b - a) for a, b in zip(edges[:-1], edges[1:])]


def kernel(
    sizes,
    w_ref,
    grad_ref,
    gate_ref,
    up_ref,
    up_out_ref,
    down_in_ref,
    out_up_ref,
    in_down_ref,
    wbuf,
    gbuf,
    gate,
    upbuf,
    acc,
    local_sem,
    up_sem,
    z_send,
    z_recv,
    y_send,
    y_recv,
    g_send,
    g_recv,
    r_send,
    r_recv,
):
    groups, dp, mp = sizes
    tokens = gate.shape[0]
    hidden_units, width = w_ref.shape
    half = width // groups
    gwidth = grad_ref.shape[1]
    pieces = cuts(hidden_units, PIECES)
    last = len(pieces) - 1
    y, z, m = (lax.axis_index(name) for name in ("groups", "dp", "mp"))
    x_count = mp // 2
    sibling = m + 1 - 2 * lax.rem(m, 2)
    has_lo, has_hi = z > 0, z < dp - 1
    tile = min(256, tokens)
    small = min(128, tokens)

    def x_peer(j):
        return lax.rem(m + 2 * j, mp)

    def y_peer(j):
        return lax.rem(y + j, groups)

    barrier = pltpu.get_barrier_semaphore()

    def greet(where):
        pl.semaphore_signal(barrier, inc=1, device_id=where, device_id_type=MESH)

    pl.when(has_lo)(lambda: greet({"dp": z - 1}))
    pl.when(has_hi)(lambda: greet({"dp": z + 1}))
    for j in range(1, groups):
        greet({"groups": y_peer(j)})
    greet({"mp": sibling})
    for j in range(1, x_count):
        greet({"mp": x_peer(j)})
    pl.semaphore_wait(
        barrier,
        has_lo.astype(jnp.int32) + has_hi.astype(jnp.int32) + (groups - 1) + 1 + (x_count - 1),
    )

    def w_slice(ref, c, part):
        start, size = pieces[c]
        return ref.at[pl.ds(start, size), pl.ds(pl.multiple_of(part * half, 128), half)]

    def z_block(way, k):
        return z + k if way == 0 else z - k

    def z_copy(way, k, c):
        block = z_block(way, k)
        return pltpu.make_async_remote_copy(
            src_ref=w_slice(w_ref if k == 0 else wbuf.at[block], c, y),
            dst_ref=w_slice(wbuf.at[block], c, y),
            send_sem=z_send.at[way, k, c],
            recv_sem=z_recv.at[block, c],
            device_id={"dp": z - 1 if way == 0 else z + 1},
            device_id_type=MESH,
        )

    def z_arrived(way, k, c):
        block = z_block(way, k)
        pltpu.make_async_remote_copy(
            src_ref=w_slice(wbuf.at[block], c, y),
            dst_ref=w_slice(wbuf.at[block], c, y),
            send_sem=z_send.at[way, k, c],
            recv_sem=z_recv.at[block, c],
            device_id={"groups": y_peer(1)},
            device_id_type=MESH,
        ).wait_recv()

    def y_copy(j, block, c, part):
        return pltpu.make_async_remote_copy(
            src_ref=w_slice(wbuf.at[block], c, part),
            dst_ref=w_slice(wbuf.at[block], c, part),
            send_sem=y_send.at[j - 1, block, c],
            recv_sem=y_recv.at[j - 1, block, c],
            device_id={"groups": y_peer(j)},
            device_id_type=MESH,
        )

    def valid(way, k):
        return (z + k <= dp - 1) if way == 0 else (z - k >= 0)

    def can_pass(way):
        return has_lo if way == 0 else has_hi

    def g_slice(ref, owner):
        return ref.at[:, pl.ds(pl.multiple_of(owner * gwidth, 128), gwidth)]

    def g_copy(where, owner, src, send, recv):
        return pltpu.make_async_remote_copy(
            src_ref=src,
            dst_ref=g_slice(gbuf, owner),
            send_sem=send,
            recv_sem=recv,
            device_id={"mp": where},
            device_id_type=MESH,
        )

    def g_first(j):
        where = sibling if j == 0 else x_peer(j)
        return g_copy(where, m, grad_ref, g_send.at[j], g_recv.at[j])

    def g_relay(j):
        owner = lax.rem(m + mp - 2 * j, mp)
        return g_copy(sibling, owner, g_slice(gbuf, owner), r_send.at[j - 1], r_recv.at[j - 1])

    for c in range(len(pieces)):
        for way in (0, 1):
            pl.when(can_pass(way))(lambda way=way, c=c: z_copy(way, 0, c).start())
    for j in range(1, x_count):
        g_first(j).start()
    g_first(0).start()

    gate_in = pltpu.make_async_copy(gate_ref, gate, local_sem.at[0])
    gate_in.start()
    w_in = pltpu.make_async_copy(w_ref, wbuf.at[z], local_sem.at[1])
    w_in.start()
    g_in = pltpu.make_async_copy(grad_ref, g_slice(gbuf, m), local_sem.at[2])
    g_in.start()
    gate_in.wait()
    w_in.wait()
    g_in.wait()

    def silu(rows, start, size):
        value = gate[rows, start : start + size].astype(jnp.float32)
        return value / (1.0 + jnp.exp(-value))

    def down_part(i):
        base = i * tile
        copy = pltpu.make_async_copy(up_ref.at[pl.ds(base, tile), :], upbuf, up_sem)
        copy.start()
        copy.wait()

        def step(t, _):
            inner = pl.ds(pl.multiple_of(t * small, small), small)
            rows = pl.ds(pl.multiple_of(base + t * small, small), small)
            total = jnp.zeros((small, in_down_ref.shape[1]), jnp.float32)
            for start, size in pieces:
                up = upbuf[inner, start : start + size].astype(jnp.float32)
                hidden = (silu(rows, start, size) * up).astype(jnp.bfloat16)
                total += jnp.dot(
                    hidden, down_in_ref[start : start + size, :], preferred_element_type=jnp.float32
                )
            in_down_ref[rows, :] = total
            return 0

        lax.fori_loop(0, tile // small, step, 0)

    def multiply(block, c, first):
        start, size = pieces[c]

        def step(t, _):
            rows = pl.ds(pl.multiple_of(t * tile, tile), tile)
            product = lax.dot_general(
                gbuf[rows, pl.ds(pl.multiple_of(block * width, 128), width)],
                wbuf[block, start : start + size, :],
                NT,
                preferred_element_type=jnp.float32,
            )
            if first:
                acc[rows, start : start + size] = product
            else:
                acc[rows, start : start + size] += product
            return 0

        lax.fori_loop(0, tokens // tile, step, 0)

    def finish(c):
        start, size = pieces[c]

        def step(t, _):
            rows = pl.ds(pl.multiple_of(t * small, small), small)
            up_grad = (acc[rows, start : start + size] * silu(rows, start, size)).astype(jnp.bfloat16)
            share = jnp.dot(
                up_grad, up_out_ref[start : start + size, :], preferred_element_type=jnp.float32
            )
            if c == 0:
                out_up_ref[rows, :] = share
            else:
                out_up_ref[rows, :] += share
            return 0

        lax.fori_loop(0, tokens // small, step, 0)

    def consume(k, c):
        if k == 0:
            multiply(z, c, True)
        else:
            for way in (0, 1):

                def one(way=way):
                    block = z_block(way, k)
                    for j in range(1, groups):
                        y_copy(j, block, c, lax.rem(y + groups - j, groups)).wait_recv()
                    multiply(block, c, False)

                pl.when(valid(way, k))(one)
        if k == dp - 1:
            finish(c)

    def gather_grad():
        g_first(0).wait_recv()
        for j in range(1, x_count):
            g_relay(j).wait_recv()

    down_todo = list(range(tokens // tile))
    todo = [(0, c) for c in range(len(pieces))]
    ready = False
    for k in range(1, dp):
        for c in range(len(pieces)):
            for way in (0, 1):

                def one(way=way):
                    z_arrived(way, k, c)
                    pl.when(can_pass(way))(lambda: z_copy(way, k, c).start())
                    block = z_block(way, k)
                    for j in range(1, groups):
                        y_copy(j, block, c, y).start()

                pl.when(valid(way, k))(one)
            if k == 1:
                if down_todo:
                    down_part(down_todo.pop(0))
                if c == last:
                    for j in range(1, x_count):
                        g_first(j).wait_recv()
                        g_relay(j).start()
            else:
                if not ready:
                    gather_grad()
                    ready = True
                for item in todo[:3]:
                    consume(*item)
                todo = todo[3:]
            todo.append((k, c))
    if not ready:
        gather_grad()
    while down_todo:
        down_part(down_todo.pop(0))
    for item in todo:
        consume(*item)

    for k in range(dp):
        for way in (0, 1):
            for c in range(len(pieces)):
                pl.when(valid(way, k) & can_pass(way))(
                    lambda way=way, c=c, k=k: z_copy(way, k, c).wait_send()
                )

                def sent(way=way, c=c, k=k):
                    for j in range(1, groups):
                        y_copy(j, z_block(way, k), c, y).wait_send()

                if k > 0:
                    pl.when(valid(way, k))(sent)
    for j in range(x_count):
        g_first(j).wait_send()
    for j in range(1, x_count):
        g_relay(j).wait_send()


def gather_and_project(sizes, down_weight, output_grad, gate, up, up_out, down_in):
    groups, dp, mp = sizes
    tokens, hidden_units = gate.shape
    rank = up_out.shape[1]
    width = down_weight.shape[1]
    count = len(cuts(hidden_units, PIECES))
    x_count = mp // 2
    tile = min(256, tokens)
    anywhere = pl.BlockSpec(memory_space=pl.ANY)
    vmem = pl.BlockSpec(memory_space=pltpu.VMEM)
    dma = pltpu.SemaphoreType.DMA
    part = jax.ShapeDtypeStruct((tokens, rank), jnp.float32)
    return pl.pallas_call(
        functools.partial(kernel, sizes),
        out_shape=(part, part),
        in_specs=[anywhere] * 4 + [vmem] * 2,
        out_specs=(vmem, vmem),
        scratch_shapes=[
            pltpu.VMEM((dp, hidden_units, width), jnp.bfloat16),
            pltpu.VMEM((tokens, output_grad.shape[1] * mp), jnp.bfloat16),
            pltpu.VMEM((tokens, hidden_units), jnp.bfloat16),
            pltpu.VMEM((tile, hidden_units), jnp.bfloat16),
            pltpu.VMEM((tokens, hidden_units), jnp.float32),
            dma((3,)),
            dma,
            dma((2, dp, count)),
            dma((dp, count)),
            dma((max(groups - 1, 1), dp, count)),
            dma((max(groups - 1, 1), dp, count)),
            dma((x_count,)),
            dma((x_count,)),
            dma((max(x_count - 1, 1),)),
            dma((max(x_count - 1, 1),)),
        ],
        compiler_params=pltpu.CompilerParams(
            collective_id=0, has_side_effects=True, vmem_limit_bytes=60 * 1024 * 1024
        ),
        cost_estimate=pl.CostEstimate(
            flops=2 * tokens * hidden_units * width * dp,
            bytes_accessed=4 * tokens * hidden_units,
            transcendentals=2 * tokens * hidden_units,
        ),
    )(down_weight, output_grad, gate, up, up_out, down_in)


def outer_sums(first, second):
    return jnp.einsum("nti,ntj->nij", first, second, precision=lax.Precision.HIGHEST)


def body(
    sizes,
    layer_input,
    output_grad,
    gate_preact,
    up_values,
    down_weight,
    up_in_factor,
    up_out_factor,
    down_in_factor,
    down_out_factor,
    queries,
):
    rank = up_in_factor.shape[1]
    count = output_grad.shape[0] // SEQ
    all_queries = lax.all_gather(queries, "dp", axis=0, tiled=True)
    early = lax.psum(
        jnp.concatenate(
            [
                jnp.dot(layer_input, up_in_factor, preferred_element_type=jnp.float32),
                jnp.dot(output_grad, down_out_factor, preferred_element_type=jnp.float32),
            ],
            1,
        ),
        "mp",
    ).reshape(count, SEQ, 2 * rank)
    out_up, in_down = gather_and_project(
        sizes, down_weight, output_grad, gate_preact, up_values, up_out_factor, down_in_factor
    )
    sketch = jnp.concatenate(
        [
            outer_sums(early[:, :, :rank], out_up.reshape(count, SEQ, rank)).reshape(count, -1),
            outer_sums(in_down.reshape(count, SEQ, rank), early[:, :, rank:]).reshape(count, -1),
        ],
        1,
    )
    scores = lax.dot_general(
        sketch,
        all_queries.astype(jnp.float32),
        NT,
        precision=lax.Precision.HIGHEST,
        preferred_element_type=jnp.float32,
    )
    return lax.psum(scores, "mp")


def solution(mesh):
    sizes = (mesh.shape["groups"], mesh.shape["dp"], mesh.shape["mp"])
    return jax.shard_map(
        functools.partial(body, sizes),
        mesh=mesh,
        in_specs=(
            P(("groups", "dp"), "mp"),
            P(("groups", "dp"), "mp"),
            P(("groups", "dp"), "mp"),
            P(("groups", "dp"), "mp"),
            P("mp", "dp"),
            P("mp", None),
            P("mp", None),
            P("mp", None),
            P("mp", None),
            P(("groups", "dp"), None),
        ),
        out_specs=P(("groups", "dp"), None),
        check_vma=False,
    )
```

```python
import functools

import jax
import jax.numpy as jnp
from jax import lax
from jax.experimental import pallas as pl
from jax.experimental.pallas import tpu as pltpu
from jax.sharding import PartitionSpec as P

SEQ = 256
SHARES = (16, 36, 46, 40, 22, 12)
MESH = pl.DeviceIdType.MESH
NT = (((1,), (1,)), ((), ()))
TN = (((0,), (0,)), ((), ()))


def cuts(total):
    units, whole, seen, edges = total // 16, sum(SHARES), 0, [0]
    for share in SHARES:
        seen += share
        edges.append(16 * (units * seen // whole))
    edges[-1] = total
    return [(a, b - a) for a, b in zip(edges[:-1], edges[1:]) if b > a]


def kernel(
    sizes,
    w_ref,
    grad_ref,
    gate_ref,
    up_ref,
    up_out_ref,
    down_in_ref,
    q_ref,
    out_up_ref,
    in_down_ref,
    all_q_ref,
    wbuf,
    gbuf,
    gate,
    upbuf,
    acc,
    local_sem,
    up_sem,
    z_send,
    z_recv,
    y_send,
    y_recv,
    g_send,
    g_recv,
    r_send,
    r_recv,
    q_send,
    q_recv,
    s_send,
    s_recv,
):
    groups, dp, mp = sizes
    tokens = gate.shape[1]
    hidden_units, width = w_ref.shape
    half = width // groups
    gwidth = grad_ref.shape[1]
    pieces = cuts(hidden_units)
    last = len(pieces) - 1
    y, z, m = (lax.axis_index(name) for name in ("groups", "dp", "mp"))
    x_count = mp // 2
    sibling = m + 1 - 2 * lax.rem(m, 2)
    has_lo, has_hi = z > 0, z < dp - 1
    tile = min(256, tokens)

    def x_peer(j):
        return lax.rem(m + 2 * j, mp)

    def m_peer(j):
        return lax.rem(m + j, mp)

    def z_peer(j):
        return lax.rem(z + j, dp)

    def y_peer(j):
        return lax.rem(y + j, groups)

    barrier = pltpu.get_barrier_semaphore()

    def greet(where):
        pl.semaphore_signal(barrier, inc=1, device_id=where, device_id_type=MESH)

    for j in range(1, dp):
        greet({"dp": z_peer(j)})
    for j in range(1, groups):
        greet({"groups": y_peer(j)})
    for j in range(1, mp):
        greet({"mp": m_peer(j)})
    pl.semaphore_wait(barrier, (dp - 1) + (groups - 1) + (mp - 1))

    def w_slice(ref, c, part):
        start, size = pieces[c]
        return ref.at[pl.ds(start, size), pl.ds(pl.multiple_of(part * half, 128), half)]

    def z_block(way, k):
        return z + k if way == 0 else z - k

    def z_copy(way, k, c):
        block = z_block(way, k)
        return pltpu.make_async_remote_copy(
            src_ref=w_slice(w_ref if k == 0 else wbuf.at[block], c, y),
            dst_ref=w_slice(wbuf.at[block], c, y),
            send_sem=z_send.at[way, k, c],
            recv_sem=z_recv.at[block, c],
            device_id={"dp": z - 1 if way == 0 else z + 1},
            device_id_type=MESH,
        )

    def z_arrived(way, k, c):
        block = z_block(way, k)
        pltpu.make_async_remote_copy(
            src_ref=w_slice(wbuf.at[block], c, y),
            dst_ref=w_slice(wbuf.at[block], c, y),
            send_sem=z_send.at[way, k, c],
            recv_sem=z_recv.at[block, c],
            device_id={"groups": y_peer(1)},
            device_id_type=MESH,
        ).wait_recv()

    def y_copy(j, block, c, part):
        return pltpu.make_async_remote_copy(
            src_ref=w_slice(wbuf.at[block], c, part),
            dst_ref=w_slice(wbuf.at[block], c, part),
            send_sem=y_send.at[j - 1, block, c],
            recv_sem=y_recv.at[j - 1, block, c],
            device_id={"groups": y_peer(j)},
            device_id_type=MESH,
        )

    def valid(way, k):
        return (z + k <= dp - 1) if way == 0 else (z - k >= 0)

    def can_pass(way):
        return has_lo if way == 0 else has_hi

    def g_slice(ref, owner):
        return ref.at[:, pl.ds(pl.multiple_of(owner * gwidth, 128), gwidth)]

    def g_copy(where, owner, src, send, recv):
        return pltpu.make_async_remote_copy(
            src_ref=src,
            dst_ref=g_slice(gbuf, owner),
            send_sem=send,
            recv_sem=recv,
            device_id={"mp": where},
            device_id_type=MESH,
        )

    def g_first(j):
        where = sibling if j == 0 else x_peer(j)
        return g_copy(where, m, grad_ref, g_send.at[j], g_recv.at[j])

    def g_relay(j):
        owner = lax.rem(m + mp - 2 * j, mp)
        return g_copy(sibling, owner, g_slice(gbuf, owner), r_send.at[j - 1], r_recv.at[j - 1])

    def q_first(j):
        return pltpu.make_async_remote_copy(
            src_ref=q_ref,
            dst_ref=all_q_ref.at[m, z],
            send_sem=q_send.at[j - 1],
            recv_sem=q_recv.at[j - 1],
            device_id={"dp": z_peer(j)},
            device_id_type=MESH,
        )

    def q_arrived(j):
        pltpu.make_async_remote_copy(
            src_ref=q_ref,
            dst_ref=all_q_ref.at[m, lax.rem(z + dp - j, dp)],
            send_sem=q_send.at[j - 1],
            recv_sem=q_recv.at[j - 1],
            device_id={"dp": z_peer(j)},
            device_id_type=MESH,
        ).wait_recv()

    def q_second(j, owner):
        return pltpu.make_async_remote_copy(
            src_ref=all_q_ref.at[owner],
            dst_ref=all_q_ref.at[owner],
            send_sem=s_send.at[j - 1],
            recv_sem=s_recv.at[j - 1],
            device_id={"mp": m_peer(j)},
            device_id_type=MESH,
        )

    for j in range(1, dp):
        q_first(j).start()
    for c in range(len(pieces)):
        for way in (0, 1):
            pl.when(can_pass(way))(lambda way=way, c=c: z_copy(way, 0, c).start())
    for j in range(1, x_count):
        g_first(j).start()
    g_first(0).start()

    gate_in = pltpu.make_async_copy(gate_ref, gate, local_sem.at[0])
    gate_in.start()
    w_in = pltpu.make_async_copy(w_ref, wbuf.at[z], local_sem.at[1])
    w_in.start()
    g_in = pltpu.make_async_copy(grad_ref, g_slice(gbuf, m), local_sem.at[2])
    g_in.start()
    q_in = pltpu.make_async_copy(q_ref, all_q_ref.at[m, z], local_sem.at[3])
    q_in.start()
    gate_in.wait()
    w_in.wait()
    g_in.wait()
    q_in.wait()

    def silu(rows, columns):
        value = gate[rows, columns].astype(jnp.float32)
        return value / (1.0 + jnp.exp(-value))

    def columns_of(t):
        return pl.ds(pl.multiple_of(t * tile, tile), tile)

    def down_part(c):
        start, size = pieces[c]
        copy = pltpu.make_async_copy(
            up_ref.at[pl.ds(start, size), :], upbuf.at[pl.ds(0, size), :], up_sem
        )
        copy.start()
        copy.wait()

        def step(t, _):
            columns = columns_of(t)
            up = upbuf[0:size, columns].astype(jnp.float32)
            hidden = (silu(pl.ds(start, size), columns) * up).astype(jnp.bfloat16)
            share = lax.dot_general(
                down_in_ref[start : start + size, :],
                hidden,
                TN,
                preferred_element_type=jnp.float32,
            )
            if c == 0:
                in_down_ref[:, columns] = share
            else:
                in_down_ref[:, columns] += share
            return 0

        lax.fori_loop(0, tokens // tile, step, 0)

    def multiply(block, c, first):
        start, size = pieces[c]

        def step(t, _):
            columns = columns_of(t)
            product = lax.dot_general(
                wbuf[block, start : start + size, :],
                gbuf[columns, pl.ds(pl.multiple_of(block * width, 128), width)],
                NT,
                preferred_element_type=jnp.float32,
            )
            if first:
                acc[start : start + size, columns] = product
            else:
                acc[start : start + size, columns] += product
            return 0

        lax.fori_loop(0, tokens // tile, step, 0)

    def finish(c):
        start, size = pieces[c]

        def step(t, _):
            columns = columns_of(t)
            up_grad = acc[start : start + size, columns] * silu(pl.ds(start, size), columns)
            share = lax.dot_general(
                up_out_ref[start : start + size, :],
                up_grad.astype(jnp.bfloat16),
                TN,
                preferred_element_type=jnp.float32,
            )
            if c == 0:
                out_up_ref[:, columns] = share
            else:
                out_up_ref[:, columns] += share
            return 0

        lax.fori_loop(0, tokens // tile, step, 0)

    def consume(k, c):
        if k == 0:
            multiply(z, c, True)
        else:
            for way in (0, 1):

                def one(way=way):
                    block = z_block(way, k)
                    for j in range(1, groups):
                        y_copy(j, block, c, lax.rem(y + groups - j, groups)).wait_recv()
                    multiply(block, c, False)

                pl.when(valid(way, k))(one)
        if k == dp - 1:
            finish(c)

    def gather_grad():
        g_first(0).wait_recv()
        for j in range(1, x_count):
            g_relay(j).wait_recv()

    down_todo = list(range(len(pieces)))
    todo = [(0, c) for c in range(len(pieces))]
    ready = False
    for k in range(1, dp):
        for c in range(len(pieces)):
            for way in (0, 1):

                def one(way=way):
                    z_arrived(way, k, c)
                    pl.when(can_pass(way))(lambda: z_copy(way, k, c).start())
                    block = z_block(way, k)
                    for j in range(1, groups):
                        y_copy(j, block, c, y).start()

                pl.when(valid(way, k))(one)
            if k == 1:
                if down_todo:
                    down_part(down_todo.pop(0))
                if c == 1:
                    for j in range(1, dp):
                        q_arrived(j)
                    for j in range(1, mp):
                        q_second(j, m).start()
                if c == last:
                    for j in range(1, x_count):
                        g_first(j).wait_recv()
                        g_relay(j).start()
            else:
                if not ready:
                    gather_grad()
                    ready = True
                for item in todo[:2]:
                    consume(*item)
                todo = todo[2:]
            todo.append((k, c))
    if not ready:
        gather_grad()
    while down_todo:
        down_part(down_todo.pop(0))
    for item in todo:
        consume(*item)

    for j in range(1, mp):
        q_second(j, lax.rem(m + mp - j, mp)).wait_recv()

    for j in range(1, dp):
        q_first(j).wait_send()
    for j in range(1, mp):
        q_second(j, m).wait_send()
    for k in range(dp):
        for way in (0, 1):
            for c in range(len(pieces)):
                pl.when(valid(way, k) & can_pass(way))(
                    lambda way=way, c=c, k=k: z_copy(way, k, c).wait_send()
                )

                def sent(way=way, c=c, k=k):
                    for j in range(1, groups):
                        y_copy(j, z_block(way, k), c, y).wait_send()

                if k > 0:
                    pl.when(valid(way, k))(sent)
    for j in range(x_count):
        g_first(j).wait_send()
    for j in range(1, x_count):
        g_relay(j).wait_send()


def gather_and_project(sizes, down_weight, output_grad, gate, up, up_out, down_in, own_queries):
    groups, dp, mp = sizes
    hidden_units, tokens = gate.shape
    rank = up_out.shape[1]
    width = down_weight.shape[1]
    pieces = cuts(hidden_units)
    count = len(pieces)
    x_count = mp // 2
    anywhere = pl.BlockSpec(memory_space=pl.ANY)
    vmem = pl.BlockSpec(memory_space=pltpu.VMEM)
    dma = pltpu.SemaphoreType.DMA
    part = jax.ShapeDtypeStruct((rank, tokens), jnp.float32)
    return pl.pallas_call(
        functools.partial(kernel, sizes),
        out_shape=(part, part, jax.ShapeDtypeStruct((mp, dp) + own_queries.shape, jnp.bfloat16)),
        in_specs=[anywhere] * 4 + [vmem] * 3,
        out_specs=(vmem, vmem, vmem),
        scratch_shapes=[
            pltpu.VMEM((dp, hidden_units, width), jnp.bfloat16),
            pltpu.VMEM((tokens, output_grad.shape[1] * mp), jnp.bfloat16),
            pltpu.VMEM((hidden_units, tokens), jnp.bfloat16),
            pltpu.VMEM((max(size for _, size in pieces), tokens), jnp.bfloat16),
            pltpu.VMEM((hidden_units, tokens), jnp.float32),
            dma((4,)),
            dma,
            dma((2, dp, count)),
            dma((dp, count)),
            dma((max(groups - 1, 1), dp, count)),
            dma((max(groups - 1, 1), dp, count)),
            dma((x_count,)),
            dma((x_count,)),
            dma((max(x_count - 1, 1),)),
            dma((max(x_count - 1, 1),)),
            dma((max(dp - 1, 1),)),
            dma((max(dp - 1, 1),)),
            dma((max(mp - 1, 1),)),
            dma((max(mp - 1, 1),)),
        ],
        compiler_params=pltpu.CompilerParams(
            collective_id=0, has_side_effects=True, vmem_limit_bytes=60 * 1024 * 1024
        ),
        cost_estimate=pl.CostEstimate(
            flops=2 * tokens * hidden_units * width * dp,
            bytes_accessed=4 * tokens * hidden_units,
            transcendentals=2 * tokens * hidden_units,
        ),
    )(down_weight, output_grad, gate, up, up_out, down_in, own_queries)


def outer_sums(first, second):
    return jnp.einsum("nti,ntj->nij", first, second, precision=lax.Precision.HIGHEST)


def body(
    sizes,
    layer_input,
    output_grad,
    gate_preact,
    up_values,
    down_weight,
    up_in_factor,
    up_out_factor,
    down_in_factor,
    down_out_factor,
    queries,
):
    groups, dp, mp = sizes
    rank = up_in_factor.shape[1]
    count = output_grad.shape[0] // SEQ
    query_rows, sketch_size = queries.shape
    share = sketch_size // mp
    own_queries = lax.dynamic_slice_in_dim(queries, lax.axis_index("mp") * share, share, 1)
    early = lax.psum(
        jnp.concatenate(
            [
                jnp.dot(layer_input, up_in_factor, preferred_element_type=jnp.float32),
                jnp.dot(output_grad, down_out_factor, preferred_element_type=jnp.float32),
            ],
            1,
        ),
        "mp",
    ).reshape(count, SEQ, 2 * rank)
    out_up, in_down, all_queries = gather_and_project(
        sizes,
        down_weight,
        output_grad,
        gate_preact.T,
        up_values.T,
        up_out_factor,
        down_in_factor,
        own_queries.reshape(query_rows * share // 128, 128),
    )
    sketch = jnp.concatenate(
        [
            jnp.einsum(
                "nti,jnt->nij",
                early[:, :, :rank],
                out_up.reshape(rank, count, SEQ),
                precision=lax.Precision.HIGHEST,
            ).reshape(count, -1),
            jnp.einsum(
                "int,ntj->nij",
                in_down.reshape(rank, count, SEQ),
                early[:, :, rank:],
                precision=lax.Precision.HIGHEST,
            ).reshape(count, -1),
        ],
        1,
    )
    scores = jnp.einsum(
        "nmc,mdqc->ndq",
        sketch.reshape(count, mp, share),
        all_queries.reshape(mp, dp, query_rows, share).astype(jnp.float32),
        precision=lax.Precision.HIGHEST,
    ).reshape(count, dp * query_rows)
    return lax.psum(scores, "mp")


def solution(mesh):
    sizes = (mesh.shape["groups"], mesh.shape["dp"], mesh.shape["mp"])
    return jax.shard_map(
        functools.partial(body, sizes),
        mesh=mesh,
        in_specs=(
            P(("groups", "dp"), "mp"),
            P(("groups", "dp"), "mp"),
            P(("groups", "dp"), "mp"),
            P(("groups", "dp"), "mp"),
            P("mp", "dp"),
            P("mp", None),
            P("mp", None),
            P("mp", None),
            P("mp", None),
            P(("groups", "dp"), None),
        ),
        out_specs=P(("groups", "dp"), None),
        check_vma=False,
    )
```

```python
import functools

import jax
import jax.numpy as jnp
from jax import lax
from jax.experimental import pallas as pl
from jax.experimental.pallas import tpu as pltpu
from jax.sharding import PartitionSpec as P

SEQ = 256
SHARES = (2, 5, 6, 5, 2, 2)
MESH = pl.DeviceIdType.MESH
NT = (((1,), (1,)), ((), ()))


def cuts(total):
    units, whole, seen, edges = -(-total // 128), sum(SHARES), 0, [0]
    for share in SHARES:
        seen += share
        edges.append(min(total, 128 * (units * seen // whole)))
    return [(a, b - a) for a, b in zip(edges[:-1], edges[1:]) if b > a]


def kernel(
    sizes,
    w_ref,
    grad_ref,
    gate_ref,
    up_ref,
    up_out_ref,
    down_in_ref,
    q_ref,
    layer_ref,
    up_in_ref,
    down_out_ref,
    sketch_ref,
    all_q_ref,
    out_up_ref,
    in_down_ref,
    early,
    parts,
    summed,
    wbuf,
    gbuf,
    gate,
    upbuf,
    acc,
    local_sem,
    up_sem,
    z_send,
    z_recv,
    y_send,
    y_recv,
    g_send,
    g_recv,
    r_send,
    r_recv,
    q_send,
    q_recv,
    s_send,
    s_recv,
    e_send,
    e_recv,
    t_send,
    t_recv,
):
    groups, dp, mp = sizes
    tokens = gate.shape[1]
    hidden_units, width = w_ref.shape
    half = width // groups
    gwidth = grad_ref.shape[1]
    pieces = cuts(hidden_units)
    last = len(pieces) - 1
    y, z, m = (lax.axis_index(name) for name in ("groups", "dp", "mp"))
    x_count = mp // 2
    sibling = m + 1 - 2 * lax.rem(m, 2)
    has_lo, has_hi = z > 0, z < dp - 1
    tile = min(256, tokens)

    def x_peer(j):
        return lax.rem(m + 2 * j, mp)

    def m_peer(j):
        return lax.rem(m + j, mp)

    def z_peer(j):
        return lax.rem(z + j, dp)

    def y_peer(j):
        return lax.rem(y + j, groups)

    barrier = pltpu.get_barrier_semaphore()

    def greet(where):
        pl.semaphore_signal(barrier, inc=1, device_id=where, device_id_type=MESH)

    for j in range(1, dp):
        greet({"dp": z_peer(j)})
    for j in range(1, groups):
        greet({"groups": y_peer(j)})
    for j in range(1, mp):
        greet({"mp": m_peer(j)})
    pl.semaphore_wait(barrier, (dp - 1) + (groups - 1) + (mp - 1))

    def w_slice(ref, c, part):
        start, size = pieces[c]
        return ref.at[pl.ds(start, size), pl.ds(pl.multiple_of(part * half, 128), half)]

    def z_block(way, k):
        return z + k if way == 0 else z - k

    def z_copy(way, k, c):
        block = z_block(way, k)
        return pltpu.make_async_remote_copy(
            src_ref=w_slice(w_ref if k == 0 else wbuf.at[block], c, y),
            dst_ref=w_slice(wbuf.at[block], c, y),
            send_sem=z_send.at[way, k, c],
            recv_sem=z_recv.at[block, c],
            device_id={"dp": z - 1 if way == 0 else z + 1},
            device_id_type=MESH,
        )

    def z_arrived(way, k, c):
        block = z_block(way, k)
        pltpu.make_async_remote_copy(
            src_ref=w_slice(wbuf.at[block], c, y),
            dst_ref=w_slice(wbuf.at[block], c, y),
            send_sem=z_send.at[way, k, c],
            recv_sem=z_recv.at[block, c],
            device_id={"groups": y_peer(1)},
            device_id_type=MESH,
        ).wait_recv()

    def y_copy(j, block, c, part):
        return pltpu.make_async_remote_copy(
            src_ref=w_slice(wbuf.at[block], c, part),
            dst_ref=w_slice(wbuf.at[block], c, part),
            send_sem=y_send.at[j - 1, block, c],
            recv_sem=y_recv.at[j - 1, block, c],
            device_id={"groups": y_peer(j)},
            device_id_type=MESH,
        )

    def valid(way, k):
        return (z + k <= dp - 1) if way == 0 else (z - k >= 0)

    def can_pass(way):
        return has_lo if way == 0 else has_hi

    def g_slice(ref, owner):
        return ref.at[:, pl.ds(pl.multiple_of(owner * gwidth, 128), gwidth)]

    def g_copy(where, owner, src, send, recv):
        return pltpu.make_async_remote_copy(
            src_ref=src,
            dst_ref=g_slice(gbuf, owner),
            send_sem=send,
            recv_sem=recv,
            device_id={"mp": where},
            device_id_type=MESH,
        )

    def g_first(j):
        where = sibling if j == 0 else x_peer(j)
        return g_copy(where, m, grad_ref, g_send.at[j], g_recv.at[j])

    def g_relay(j):
        owner = lax.rem(m + mp - 2 * j, mp)
        return g_copy(sibling, owner, g_slice(gbuf, owner), r_send.at[j - 1], r_recv.at[j - 1])

    def q_first(j):
        return pltpu.make_async_remote_copy(
            src_ref=q_ref,
            dst_ref=all_q_ref.at[m, z],
            send_sem=q_send.at[j - 1],
            recv_sem=q_recv.at[j - 1],
            device_id={"dp": z_peer(j)},
            device_id_type=MESH,
        )

    def q_arrived(j):
        pltpu.make_async_remote_copy(
            src_ref=q_ref,
            dst_ref=all_q_ref.at[m, lax.rem(z + dp - j, dp)],
            send_sem=q_send.at[j - 1],
            recv_sem=q_recv.at[j - 1],
            device_id={"dp": z_peer(j)},
            device_id_type=MESH,
        ).wait_recv()

    def q_second(j, owner):
        return pltpu.make_async_remote_copy(
            src_ref=all_q_ref.at[owner],
            dst_ref=all_q_ref.at[owner],
            send_sem=s_send.at[j - 1],
            recv_sem=s_recv.at[j - 1],
            device_id={"mp": m_peer(j)},
            device_id_type=MESH,
        )

    for j in range(1, dp):
        q_first(j).start()
    for c in range(len(pieces)):
        for way in (0, 1):
            pl.when(can_pass(way))(lambda way=way, c=c: z_copy(way, 0, c).start())
    for j in range(1, x_count):
        g_first(j).start()
    g_first(0).start()

    gate_in = pltpu.make_async_copy(gate_ref, gate, local_sem.at[0])
    gate_in.start()
    w_in = pltpu.make_async_copy(w_ref, wbuf.at[z], local_sem.at[1])
    w_in.start()
    g_in = pltpu.make_async_copy(grad_ref, g_slice(gbuf, m), local_sem.at[2])
    g_in.start()
    q_in = pltpu.make_async_copy(q_ref, all_q_ref.at[m, z], local_sem.at[3])
    q_in.start()
    gate_in.wait()
    w_in.wait()
    g_in.wait()
    q_in.wait()

    def silu(rows, columns):
        value = gate[rows, columns].astype(jnp.float32)
        return value / (1.0 + jnp.exp(-value))

    def columns_of(t):
        return pl.ds(pl.multiple_of(t * tile, tile), tile)

    rank = up_in_ref.shape[0]
    share_rows = 2 * rank // mp

    def early_rows(owner):
        return pl.ds(pl.multiple_of(owner * share_rows, 8), share_rows)

    def early_part():
        room = min(tokens, upbuf.shape[0])
        for first in range(0, tokens, room):
            count = min(room, tokens - first)
            copy = pltpu.make_async_copy(
                layer_ref.at[pl.ds(first, count), :],
                upbuf.at[pl.ds(0, count), pl.ds(0, gwidth)],
                up_sem,
            )
            copy.start()
            copy.wait()
            early[0:rank, first : first + count] = lax.dot_general(
                up_in_ref[...], upbuf[0:count, 0:gwidth], NT, preferred_element_type=jnp.float32
            )

        def step(t, _):
            columns = columns_of(t)
            early[rank : 2 * rank, columns] = lax.dot_general(
                down_out_ref[...],
                gbuf[columns, pl.ds(pl.multiple_of(m * gwidth, 128), gwidth)],
                NT,
                preferred_element_type=jnp.float32,
            )
            return 0

        lax.fori_loop(0, tokens // tile, step, 0)

    def early_out(j):
        return pltpu.make_async_remote_copy(
            src_ref=early.at[early_rows(m_peer(j))],
            dst_ref=parts.at[j - 1],
            send_sem=e_send.at[j - 1],
            recv_sem=e_recv.at[j - 1],
            device_id={"mp": m_peer(j)},
            device_id_type=MESH,
        )

    def early_back(j, owner):
        return pltpu.make_async_remote_copy(
            src_ref=summed.at[early_rows(owner)],
            dst_ref=summed.at[early_rows(owner)],
            send_sem=t_send.at[j - 1],
            recv_sem=t_recv.at[j - 1],
            device_id={"mp": m_peer(j)},
            device_id_type=MESH,
        )

    def early_sum():
        rows = early_rows(m)
        total = early[rows, :]
        for j in range(1, mp):
            early_out(j).wait_recv()
            total += parts[j - 1]
        summed[rows, :] = total
        for j in range(1, mp):
            early_back(j, m).start()

    def down_part(c):
        start, size = pieces[c]
        copy = pltpu.make_async_copy(
            up_ref.at[pl.ds(start, size), :], upbuf.at[pl.ds(0, size), :], up_sem
        )
        copy.start()
        copy.wait()

        def step(t, _):
            columns = columns_of(t)
            up = upbuf[0:size, columns].astype(jnp.float32)
            hidden = (silu(pl.ds(start, size), columns) * up).astype(jnp.bfloat16)
            share = jnp.dot(
                down_in_ref[:, start : start + size], hidden, preferred_element_type=jnp.float32
            )
            if c == 0:
                in_down_ref[:, columns] = share
            else:
                in_down_ref[:, columns] += share
            return 0

        lax.fori_loop(0, tokens // tile, step, 0)

    def multiply(block, c, first):
        start, size = pieces[c]

        def step(t, _):
            columns = columns_of(t)
            product = lax.dot_general(
                wbuf[block, start : start + size, :],
                gbuf[columns, pl.ds(pl.multiple_of(block * width, 128), width)],
                NT,
                preferred_element_type=jnp.float32,
            )
            if first:
                acc[start : start + size, columns] = product
            else:
                acc[start : start + size, columns] += product
            return 0

        lax.fori_loop(0, tokens // tile, step, 0)

    def finish(c):
        start, size = pieces[c]

        def step(t, _):
            columns = columns_of(t)
            up_grad = acc[start : start + size, columns] * silu(pl.ds(start, size), columns)
            share = jnp.dot(
                up_out_ref[:, start : start + size],
                up_grad.astype(jnp.bfloat16),
                preferred_element_type=jnp.float32,
            )
            if c == 0:
                out_up_ref[:, columns] = share
            else:
                out_up_ref[:, columns] += share
            return 0

        lax.fori_loop(0, tokens // tile, step, 0)

    def consume(k, c):
        if k == 0:
            multiply(z, c, True)
        else:
            for way in (0, 1):

                def one(way=way):
                    block = z_block(way, k)
                    for j in range(1, groups):
                        y_copy(j, block, c, lax.rem(y + groups - j, groups)).wait_recv()
                    multiply(block, c, False)

                pl.when(valid(way, k))(one)
        if k == dp - 1:
            finish(c)

    def gather_grad():
        g_first(0).wait_recv()
        for j in range(1, x_count):
            g_relay(j).wait_recv()

    down_todo = list(range(len(pieces)))
    todo = [(0, c) for c in range(len(pieces))]
    ready = False
    for k in range(1, dp):
        for c in range(len(pieces)):
            for way in (0, 1):

                def one(way=way):
                    z_arrived(way, k, c)
                    pl.when(can_pass(way))(lambda: z_copy(way, k, c).start())
                    block = z_block(way, k)
                    for j in range(1, groups):
                        y_copy(j, block, c, y).start()

                pl.when(valid(way, k))(one)
            if k == 1:
                if down_todo:
                    down_part(down_todo.pop(0))
                if c == 0:
                    early_part()
                    for j in range(1, mp):
                        early_out(j).start()
                if c == 2:
                    early_sum()
                if c == 1:
                    for j in range(1, dp):
                        q_arrived(j)
                    for j in range(1, mp):
                        q_second(j, m).start()
                if c == last:
                    for j in range(1, x_count):
                        g_first(j).wait_recv()
                        g_relay(j).start()
            else:
                if not ready:
                    gather_grad()
                    ready = True
                for item in todo[:2]:
                    consume(*item)
                todo = todo[2:]
            todo.append((k, c))
    if not ready:
        gather_grad()
    while down_todo:
        down_part(down_todo.pop(0))
    for item in todo:
        consume(*item)

    for j in range(1, mp):
        q_second(j, lax.rem(m + mp - j, mp)).wait_recv()

    for j in range(1, mp):
        early_back(j, lax.rem(m + mp - j, mp)).wait_recv()

    for n in range(tokens // SEQ):
        own = pl.ds(n * SEQ, SEQ)
        for part, (first, second) in enumerate(
            (
                (summed[0:rank, own], out_up_ref[:, own]),
                (in_down_ref[:, own], summed[rank : 2 * rank, own]),
            )
        ):
            sketch_ref[n, part * rank : (part + 1) * rank, :] = lax.dot_general(
                first,
                second,
                NT,
                precision=lax.Precision.HIGHEST,
                preferred_element_type=jnp.float32,
            )

    for j in range(1, mp):
        early_out(j).wait_send()
        early_back(j, m).wait_send()
    for j in range(1, dp):
        q_first(j).wait_send()
    for j in range(1, mp):
        q_second(j, m).wait_send()
    for k in range(dp):
        for way in (0, 1):
            for c in range(len(pieces)):
                pl.when(valid(way, k) & can_pass(way))(
                    lambda way=way, c=c, k=k: z_copy(way, k, c).wait_send()
                )

                def sent(way=way, c=c, k=k):
                    for j in range(1, groups):
                        y_copy(j, z_block(way, k), c, y).wait_send()

                if k > 0:
                    pl.when(valid(way, k))(sent)
    for j in range(x_count):
        g_first(j).wait_send()
    for j in range(1, x_count):
        g_relay(j).wait_send()


def gather_and_project(
    sizes,
    down_weight,
    output_grad,
    gate,
    up,
    up_out,
    down_in,
    own_queries,
    layer_input,
    up_in,
    down_out,
):
    groups, dp, mp = sizes
    hidden_units, tokens = gate.shape
    rank = up_out.shape[0]
    width = down_weight.shape[1]
    pieces = cuts(hidden_units)
    count = len(pieces)
    x_count = mp // 2
    anywhere = pl.BlockSpec(memory_space=pl.ANY)
    vmem = pl.BlockSpec(memory_space=pltpu.VMEM)
    dma = pltpu.SemaphoreType.DMA
    gwidth = output_grad.shape[1]
    return pl.pallas_call(
        functools.partial(kernel, sizes),
        out_shape=(
            jax.ShapeDtypeStruct((tokens // SEQ, 2 * rank, rank), jnp.float32),
            jax.ShapeDtypeStruct((mp, dp) + own_queries.shape, jnp.bfloat16),
        ),
        in_specs=[anywhere] * 4 + [vmem] * 3 + [anywhere] + [vmem] * 2,
        out_specs=(vmem, vmem),
        scratch_shapes=[
            pltpu.VMEM((rank, tokens), jnp.float32),
            pltpu.VMEM((rank, tokens), jnp.float32),
            pltpu.VMEM((2 * rank, tokens), jnp.float32),
            pltpu.VMEM((max(mp - 1, 1), 2 * rank // mp, tokens), jnp.float32),
            pltpu.VMEM((2 * rank, tokens), jnp.float32),
            pltpu.VMEM((dp, hidden_units, width), jnp.bfloat16),
            pltpu.VMEM((tokens, output_grad.shape[1] * mp), jnp.bfloat16),
            pltpu.VMEM((hidden_units, tokens), jnp.bfloat16),
            pltpu.VMEM((max(size for _, size in pieces), max(tokens, gwidth)), jnp.bfloat16),
            pltpu.VMEM((hidden_units, tokens), jnp.float32),
            dma((4,)),
            dma,
            dma((2, dp, count)),
            dma((dp, count)),
            dma((max(groups - 1, 1), dp, count)),
            dma((max(groups - 1, 1), dp, count)),
            dma((x_count,)),
            dma((x_count,)),
            dma((max(x_count - 1, 1),)),
            dma((max(x_count - 1, 1),)),
            dma((max(dp - 1, 1),)),
            dma((max(dp - 1, 1),)),
        ]
        + [dma((max(mp - 1, 1),))] * 6,
        compiler_params=pltpu.CompilerParams(
            collective_id=0, has_side_effects=True, vmem_limit_bytes=60 * 1024 * 1024
        ),
        cost_estimate=pl.CostEstimate(
            flops=2 * tokens * hidden_units * width * dp,
            bytes_accessed=4 * tokens * hidden_units,
            transcendentals=2 * tokens * hidden_units,
        ),
    )(
        down_weight,
        output_grad,
        gate,
        up,
        up_out,
        down_in,
        own_queries,
        layer_input,
        up_in,
        down_out,
    )


def body(
    sizes,
    layer_input,
    output_grad,
    gate_preact,
    up_values,
    down_weight,
    up_in_factor,
    up_out_factor,
    down_in_factor,
    down_out_factor,
    queries,
):
    groups, dp, mp = sizes
    count = output_grad.shape[0] // SEQ
    query_rows, sketch_size = queries.shape
    share = sketch_size // mp
    own_queries = lax.dynamic_slice_in_dim(queries, lax.axis_index("mp") * share, share, 1)
    sketch, all_queries = gather_and_project(
        sizes,
        down_weight,
        output_grad,
        gate_preact.T,
        up_values.T,
        up_out_factor.T,
        down_in_factor.T,
        own_queries.reshape(query_rows * share // 128, 128),
        layer_input,
        up_in_factor.T,
        down_out_factor.T,
    )
    scores = jnp.einsum(
        "nmc,mdqc->ndq",
        sketch.reshape(count, mp, share),
        all_queries.reshape(mp, dp, query_rows, share).astype(jnp.float32),
        precision=lax.Precision.HIGHEST,
    ).reshape(count, dp * query_rows)
    return lax.psum(scores, "mp")


def solution(mesh):
    sizes = (mesh.shape["groups"], mesh.shape["dp"], mesh.shape["mp"])
    return jax.shard_map(
        functools.partial(body, sizes),
        mesh=mesh,
        in_specs=(
            P(("groups", "dp"), "mp"),
            P(("groups", "dp"), "mp"),
            P(("groups", "dp"), "mp"),
            P(("groups", "dp"), "mp"),
            P("mp", "dp"),
            P("mp", None),
            P("mp", None),
            P("mp", None),
            P("mp", None),
            P(("groups", "dp"), None),
        ),
        out_specs=P(("groups", "dp"), None),
        check_vma=False,
    )
```

```python
import functools

import jax
import jax.numpy as jnp
from jax import lax
from jax.experimental import pallas as pl
from jax.experimental.pallas import tpu as pltpu
from jax.sharding import PartitionSpec as P

SEQ = 256
SHARES = (1, 4, 6, 6, 4, 1)
MESH = pl.DeviceIdType.MESH
NT = (((1,), (1,)), ((), ()))


def cuts(total):
    units, whole, seen, edges = -(-total // 128), sum(SHARES), 0, [0]
    for share in SHARES:
        seen += share
        edges.append(min(total, 128 * (units * seen // whole)))
    return [(a, b - a) for a, b in zip(edges[:-1], edges[1:]) if b > a]


def kernel(
    sizes,
    w_ref,
    grad_ref,
    gate_ref,
    up_ref,
    up_out_ref,
    down_in_ref,
    q_ref,
    layer_ref,
    up_in_ref,
    down_out_ref,
    sketch_ref,
    all_q_ref,
    out_up_ref,
    in_down_ref,
    early,
    parts,
    summed,
    wbuf,
    gbuf,
    gate,
    upbuf,
    acc,
    local_sem,
    up_sem,
    z_send,
    z_recv,
    y_send,
    y_recv,
    g_send,
    g_recv,
    r_send,
    r_recv,
    q_send,
    q_recv,
    s_send,
    s_recv,
    e_send,
    e_recv,
    t_send,
    t_recv,
):
    groups, dp, mp = sizes
    tokens = gate.shape[1]
    hidden_units, width = w_ref.shape
    half = width // groups
    gwidth = grad_ref.shape[1]
    pieces = cuts(hidden_units)
    last = len(pieces) - 1
    y, z, m = (lax.axis_index(name) for name in ("groups", "dp", "mp"))
    x_count = mp // 2
    sibling = m + 1 - 2 * lax.rem(m, 2)
    has_lo, has_hi = z > 0, z < dp - 1
    tile = min(256, tokens)

    def x_peer(j):
        return lax.rem(m + 2 * j, mp)

    def m_peer(j):
        return lax.rem(m + j, mp)

    def z_peer(j):
        return lax.rem(z + j, dp)

    def y_peer(j):
        return lax.rem(y + j, groups)

    barrier = pltpu.get_barrier_semaphore()

    def greet(where):
        pl.semaphore_signal(barrier, inc=1, device_id=where, device_id_type=MESH)

    for j in range(1, dp):
        greet({"dp": z_peer(j)})
    for j in range(1, groups):
        greet({"groups": y_peer(j)})
    for j in range(1, mp):
        greet({"mp": m_peer(j)})
    pl.semaphore_wait(barrier, (dp - 1) + (groups - 1) + (mp - 1))

    def w_slice(ref, c, part):
        start, size = pieces[c]
        return ref.at[pl.ds(start, size), pl.ds(pl.multiple_of(part * half, 128), half)]

    def z_block(way, k):
        return z + k if way == 0 else z - k

    def z_copy(way, k, c):
        block = z_block(way, k)
        return pltpu.make_async_remote_copy(
            src_ref=w_slice(w_ref if k == 0 else wbuf.at[block], c, y),
            dst_ref=w_slice(wbuf.at[block], c, y),
            send_sem=z_send.at[way, k, c],
            recv_sem=z_recv.at[block, c],
            device_id={"dp": z - 1 if way == 0 else z + 1},
            device_id_type=MESH,
        )

    def z_arrived(way, k, c):
        block = z_block(way, k)
        pltpu.make_async_remote_copy(
            src_ref=w_slice(wbuf.at[block], c, y),
            dst_ref=w_slice(wbuf.at[block], c, y),
            send_sem=z_send.at[way, k, c],
            recv_sem=z_recv.at[block, c],
            device_id={"groups": y_peer(1)},
            device_id_type=MESH,
        ).wait_recv()

    def y_copy(j, block, c, part):
        return pltpu.make_async_remote_copy(
            src_ref=w_slice(wbuf.at[block], c, part),
            dst_ref=w_slice(wbuf.at[block], c, part),
            send_sem=y_send.at[j - 1, block, c],
            recv_sem=y_recv.at[j - 1, block, c],
            device_id={"groups": y_peer(j)},
            device_id_type=MESH,
        )

    def valid(way, k):
        return (z + k <= dp - 1) if way == 0 else (z - k >= 0)

    def can_pass(way):
        return has_lo if way == 0 else has_hi

    def g_slice(ref, owner):
        return ref.at[:, pl.ds(pl.multiple_of(owner * gwidth, 128), gwidth)]

    def g_copy(where, owner, src, send, recv):
        return pltpu.make_async_remote_copy(
            src_ref=src,
            dst_ref=g_slice(gbuf, owner),
            send_sem=send,
            recv_sem=recv,
            device_id={"mp": where},
            device_id_type=MESH,
        )

    def g_first(j):
        where = sibling if j == 0 else x_peer(j)
        return g_copy(where, m, grad_ref, g_send.at[j], g_recv.at[j])

    def g_relay(j):
        owner = lax.rem(m + mp - 2 * j, mp)
        return g_copy(sibling, owner, g_slice(gbuf, owner), r_send.at[j - 1], r_recv.at[j - 1])

    def q_first(j):
        return pltpu.make_async_remote_copy(
            src_ref=q_ref,
            dst_ref=all_q_ref.at[m, z],
            send_sem=q_send.at[j - 1],
            recv_sem=q_recv.at[j - 1],
            device_id={"dp": z_peer(j)},
            device_id_type=MESH,
        )

    def q_arrived(j):
        pltpu.make_async_remote_copy(
            src_ref=q_ref,
            dst_ref=all_q_ref.at[m, lax.rem(z + dp - j, dp)],
            send_sem=q_send.at[j - 1],
            recv_sem=q_recv.at[j - 1],
            device_id={"dp": z_peer(j)},
            device_id_type=MESH,
        ).wait_recv()

    def q_second(j, owner):
        return pltpu.make_async_remote_copy(
            src_ref=all_q_ref.at[owner],
            dst_ref=all_q_ref.at[owner],
            send_sem=s_send.at[j - 1],
            recv_sem=s_recv.at[j - 1],
            device_id={"mp": m_peer(j)},
            device_id_type=MESH,
        )

    for j in range(1, dp):
        q_first(j).start()
    for c in range(len(pieces)):
        for way in (0, 1):
            pl.when(can_pass(way))(lambda way=way, c=c: z_copy(way, 0, c).start())
    for j in range(1, x_count):
        g_first(j).start()
    g_first(0).start()

    gate_in = pltpu.make_async_copy(gate_ref, gate, local_sem.at[0])
    gate_in.start()
    w_in = pltpu.make_async_copy(w_ref, wbuf.at[z], local_sem.at[1])
    w_in.start()
    g_in = pltpu.make_async_copy(grad_ref, g_slice(gbuf, m), local_sem.at[2])
    g_in.start()
    q_in = pltpu.make_async_copy(q_ref, all_q_ref.at[m, z], local_sem.at[3])
    q_in.start()
    gate_in.wait()
    w_in.wait()
    g_in.wait()
    q_in.wait()

    def silu(rows, columns):
        value = gate[rows, columns].astype(jnp.float32)
        return value / (1.0 + jnp.exp(-value))

    def columns_of(t):
        return pl.ds(pl.multiple_of(t * tile, tile), tile)

    rank = up_in_ref.shape[0]
    share_rows = 2 * rank // mp

    def early_rows(owner):
        return pl.ds(pl.multiple_of(owner * share_rows, 8), share_rows)

    def early_part():
        room = min(tokens, upbuf.shape[0])
        for first in range(0, tokens, room):
            count = min(room, tokens - first)
            copy = pltpu.make_async_copy(
                layer_ref.at[pl.ds(first, count), :],
                upbuf.at[pl.ds(0, count), pl.ds(0, gwidth)],
                up_sem,
            )
            copy.start()
            copy.wait()
            early[0:rank, first : first + count] = lax.dot_general(
                up_in_ref[...], upbuf[0:count, 0:gwidth], NT, preferred_element_type=jnp.float32
            )

        def step(t, _):
            columns = columns_of(t)
            early[rank : 2 * rank, columns] = lax.dot_general(
                down_out_ref[...],
                gbuf[columns, pl.ds(pl.multiple_of(m * gwidth, 128), gwidth)],
                NT,
                preferred_element_type=jnp.float32,
            )
            return 0

        lax.fori_loop(0, tokens // tile, step, 0)

    def early_out(j):
        return pltpu.make_async_remote_copy(
            src_ref=early.at[early_rows(m_peer(j))],
            dst_ref=parts.at[j - 1],
            send_sem=e_send.at[j - 1],
            recv_sem=e_recv.at[j - 1],
            device_id={"mp": m_peer(j)},
            device_id_type=MESH,
        )

    def early_back(j, owner):
        return pltpu.make_async_remote_copy(
            src_ref=summed.at[early_rows(owner)],
            dst_ref=summed.at[early_rows(owner)],
            send_sem=t_send.at[j - 1],
            recv_sem=t_recv.at[j - 1],
            device_id={"mp": m_peer(j)},
            device_id_type=MESH,
        )

    def early_sum():
        rows = early_rows(m)
        total = early[rows, :]
        for j in range(1, mp):
            early_out(j).wait_recv()
            total += parts[j - 1]
        summed[rows, :] = total
        for j in range(1, mp):
            early_back(j, m).start()

    def down_part(c):
        start, size = pieces[c]
        copy = pltpu.make_async_copy(
            up_ref.at[pl.ds(start, size), :], upbuf.at[pl.ds(0, size), :], up_sem
        )
        copy.start()
        copy.wait()

        def step(t, _):
            columns = columns_of(t)
            up = upbuf[0:size, columns].astype(jnp.float32)
            hidden = (silu(pl.ds(start, size), columns) * up).astype(jnp.bfloat16)
            share = jnp.dot(
                down_in_ref[:, start : start + size], hidden, preferred_element_type=jnp.float32
            )
            if c == 0:
                in_down_ref[:, columns] = share
            else:
                in_down_ref[:, columns] += share
            return 0

        lax.fori_loop(0, tokens // tile, step, 0)

    def multiply(block, c, first):
        start, size = pieces[c]

        def step(t, _):
            columns = columns_of(t)
            product = lax.dot_general(
                wbuf[block, start : start + size, :],
                gbuf[columns, pl.ds(pl.multiple_of(block * width, 128), width)],
                NT,
                preferred_element_type=jnp.float32,
            )
            if first:
                acc[start : start + size, columns] = product
            else:
                acc[start : start + size, columns] += product
            return 0

        lax.fori_loop(0, tokens // tile, step, 0)

    def finish(c):
        start, size = pieces[c]

        def step(t, _):
            columns = columns_of(t)
            up_grad = acc[start : start + size, columns] * silu(pl.ds(start, size), columns)
            share = jnp.dot(
                up_out_ref[:, start : start + size],
                up_grad.astype(jnp.bfloat16),
                preferred_element_type=jnp.float32,
            )
            if c == 0:
                out_up_ref[:, columns] = share
            else:
                out_up_ref[:, columns] += share
            return 0

        lax.fori_loop(0, tokens // tile, step, 0)

    def consume(k, c):
        if k == 0:
            multiply(z, c, True)
        else:
            for way in (0, 1):

                def one(way=way):
                    block = z_block(way, k)
                    for j in range(1, groups):
                        y_copy(j, block, c, lax.rem(y + groups - j, groups)).wait_recv()
                    multiply(block, c, False)

                pl.when(valid(way, k))(one)
        if k == dp - 1:
            finish(c)

    def gather_grad():
        g_first(0).wait_recv()
        for j in range(1, x_count):
            g_relay(j).wait_recv()

    down_todo = list(range(len(pieces)))
    todo = [(0, c) for c in range(len(pieces))]
    ready = False
    for k in range(1, dp):
        for c in range(len(pieces)):
            for way in (0, 1):

                def one(way=way):
                    z_arrived(way, k, c)
                    pl.when(can_pass(way))(lambda: z_copy(way, k, c).start())
                    block = z_block(way, k)
                    for j in range(1, groups):
                        y_copy(j, block, c, y).start()

                pl.when(valid(way, k))(one)
            if k == 1:
                if down_todo:
                    down_part(down_todo.pop(0))
                if c == 0:
                    early_part()
                    for j in range(1, mp):
                        early_out(j).start()
                if c == 2:
                    early_sum()
                if c == 1:
                    for j in range(1, dp):
                        q_arrived(j)
                    for j in range(1, mp):
                        q_second(j, m).start()
                if c == last:
                    for j in range(1, x_count):
                        g_first(j).wait_recv()
                        g_relay(j).start()
            else:
                if not ready:
                    gather_grad()
                    ready = True
                for item in todo[:2]:
                    consume(*item)
                todo = todo[2:]
            todo.append((k, c))
    if not ready:
        gather_grad()
    while down_todo:
        down_part(down_todo.pop(0))
    for item in todo:
        consume(*item)

    for j in range(1, mp):
        q_second(j, lax.rem(m + mp - j, mp)).wait_recv()

    for j in range(1, mp):
        early_back(j, lax.rem(m + mp - j, mp)).wait_recv()

    for n in range(tokens // SEQ):
        own = pl.ds(n * SEQ, SEQ)
        for part, (first, second) in enumerate(
            (
                (summed[0:rank, own], out_up_ref[:, own]),
                (in_down_ref[:, own], summed[rank : 2 * rank, own]),
            )
        ):
            sketch_ref[n, part * rank : (part + 1) * rank, :] = lax.dot_general(
                first,
                second,
                NT,
                precision=lax.Precision.HIGHEST,
                preferred_element_type=jnp.float32,
            )

    for j in range(1, mp):
        early_out(j).wait_send()
        early_back(j, m).wait_send()
    for j in range(1, dp):
        q_first(j).wait_send()
    for j in range(1, mp):
        q_second(j, m).wait_send()
    for k in range(dp):
        for way in (0, 1):
            for c in range(len(pieces)):
                pl.when(valid(way, k) & can_pass(way))(
                    lambda way=way, c=c, k=k: z_copy(way, k, c).wait_send()
                )

                def sent(way=way, c=c, k=k):
                    for j in range(1, groups):
                        y_copy(j, z_block(way, k), c, y).wait_send()

                if k > 0:
                    pl.when(valid(way, k))(sent)
    for j in range(x_count):
        g_first(j).wait_send()
    for j in range(1, x_count):
        g_relay(j).wait_send()


def gather_and_project(
    sizes,
    down_weight,
    output_grad,
    gate,
    up,
    up_out,
    down_in,
    own_queries,
    layer_input,
    up_in,
    down_out,
):
    groups, dp, mp = sizes
    hidden_units, tokens = gate.shape
    rank = up_out.shape[0]
    width = down_weight.shape[1]
    pieces = cuts(hidden_units)
    count = len(pieces)
    x_count = mp // 2
    anywhere = pl.BlockSpec(memory_space=pl.ANY)
    vmem = pl.BlockSpec(memory_space=pltpu.VMEM)
    dma = pltpu.SemaphoreType.DMA
    gwidth = output_grad.shape[1]
    return pl.pallas_call(
        functools.partial(kernel, sizes),
        out_shape=(
            jax.ShapeDtypeStruct((tokens // SEQ, 2 * rank, rank), jnp.float32),
            jax.ShapeDtypeStruct((mp, dp) + own_queries.shape, jnp.bfloat16),
        ),
        in_specs=[anywhere] * 4 + [vmem] * 3 + [anywhere] + [vmem] * 2,
        out_specs=(vmem, vmem),
        scratch_shapes=[
            pltpu.VMEM((rank, tokens), jnp.float32),
            pltpu.VMEM((rank, tokens), jnp.float32),
            pltpu.VMEM((2 * rank, tokens), jnp.float32),
            pltpu.VMEM((max(mp - 1, 1), 2 * rank // mp, tokens), jnp.float32),
            pltpu.VMEM((2 * rank, tokens), jnp.float32),
            pltpu.VMEM((dp, hidden_units, width), jnp.bfloat16),
            pltpu.VMEM((tokens, output_grad.shape[1] * mp), jnp.bfloat16),
            pltpu.VMEM((hidden_units, tokens), jnp.bfloat16),
            pltpu.VMEM((max(size for _, size in pieces), max(tokens, gwidth)), jnp.bfloat16),
            pltpu.VMEM((hidden_units, tokens), jnp.float32),
            dma((4,)),
            dma,
            dma((2, dp, count)),
            dma((dp, count)),
            dma((max(groups - 1, 1), dp, count)),
            dma((max(groups - 1, 1), dp, count)),
            dma((x_count,)),
            dma((x_count,)),
            dma((max(x_count - 1, 1),)),
            dma((max(x_count - 1, 1),)),
            dma((max(dp - 1, 1),)),
            dma((max(dp - 1, 1),)),
        ]
        + [dma((max(mp - 1, 1),))] * 6,
        compiler_params=pltpu.CompilerParams(
            collective_id=0, has_side_effects=True, vmem_limit_bytes=60 * 1024 * 1024
        ),
        cost_estimate=pl.CostEstimate(
            flops=2 * tokens * hidden_units * width * dp,
            bytes_accessed=4 * tokens * hidden_units,
            transcendentals=2 * tokens * hidden_units,
        ),
    )(
        down_weight,
        output_grad,
        gate,
        up,
        up_out,
        down_in,
        own_queries,
        layer_input,
        up_in,
        down_out,
    )


def body(
    sizes,
    layer_input,
    output_grad,
    gate_preact,
    up_values,
    down_weight,
    up_in_factor,
    up_out_factor,
    down_in_factor,
    down_out_factor,
    queries,
):
    groups, dp, mp = sizes
    count = output_grad.shape[0] // SEQ
    query_rows, sketch_size = queries.shape
    share = sketch_size // mp
    own_queries = lax.dynamic_slice_in_dim(queries, lax.axis_index("mp") * share, share, 1)
    sketch, all_queries = gather_and_project(
        sizes,
        down_weight,
        output_grad,
        gate_preact.T,
        up_values.T,
        up_out_factor.T,
        down_in_factor.T,
        own_queries.reshape(query_rows * share // 128, 128),
        layer_input,
        up_in_factor.T,
        down_out_factor.T,
    )
    scores = jnp.einsum(
        "nmc,mdqc->ndq",
        sketch.reshape(count, mp, share),
        all_queries.reshape(mp, dp, query_rows, share).astype(jnp.float32),
        precision=lax.Precision.HIGHEST,
    ).reshape(count, dp * query_rows)
    return lax.psum(scores, "mp")


def solution(mesh):
    sizes = (mesh.shape["groups"], mesh.shape["dp"], mesh.shape["mp"])
    return jax.shard_map(
        functools.partial(body, sizes),
        mesh=mesh,
        in_specs=(
            P(("groups", "dp"), "mp"),
            P(("groups", "dp"), "mp"),
            P(("groups", "dp"), "mp"),
            P(("groups", "dp"), "mp"),
            P("mp", "dp"),
            P("mp", None),
            P("mp", None),
            P("mp", None),
            P("mp", None),
            P(("groups", "dp"), None),
        ),
        out_specs=P(("groups", "dp"), None),
        check_vma=False,
    )
```
